32 devices in a mesh: dp: 4 (over z), expert: 8 (over y, x, core).
Axes of the slice: x: 2, y: 2, z: 4, core: 2. Of those that a mesh axis runs over, the one named last changes fastest.
Arguments:
- tokens: bfloat16 [5120, 2048], P(('dp', 'expert')), may hold values from -6 to 6
- target: bfloat16 [5120, 2048], P(('dp', 'expert')), may hold values from -6 to 6
- expert_ids: int32 [5120, 4], P(('dp', 'expert')), may hold values from 0 to 15, all different within a row; in each aligned block of 160 rows (0 to 159, 160 to 319, ...) at most 60 rows name the same one
- gates: float32 [5120, 4], P(('dp', 'expert')), may hold values from 0.05 to 0.5
- w_in: bfloat16 [2048, 16, 1536], P(None, 'expert'), may hold values from -0.125 to 0.125
- w_out: bfloat16 [768, 16, 2048], P(None, 'expert'), may hold values from -0.21875 to 0.21875
Outputs:
- grad_tokens: bfloat16 [5120, 2048], P(('dp', 'expert'))
- grad_in: bfloat16 [2048, 16, 1536], P('dp', 'expert')
- grad_out: bfloat16 [768, 16, 2048], P(None, 'expert', 'dp')
The draws below stay inside these ranges and needn't reach their ends.
Inputs may be any that keep to these rules, and one draw needn't show every extreme that they name: `expert_ids`: each token names 4 different experts; in each aligned block of 160 rows (the tokens of one device) no expert is named by more than 60 rows, a bound that some block reaches.
All inputs are finite; a program needn't handle non-finite values.
Results may differ from the reference program's by a relative error of at most 0.012.
Values may be sent and summed in bfloat16 or wider, within the bound.
A program may use at most 192 MiB of HBM per device.

```python
import math
import jax
import jax.numpy as jnp
import numpy as np
from jax import lax

D = 2048
H = 768
TOPK = 4
TOK_DEV = 160
EXPERTS = 16
CAP = 60
TOKENS = 5120
N_DP = 4
N_EXPERT = 8


def block_levels(own_key, shape, cuts, smallest, top_value):
    loudness, own = 1.0, jax.random.fold_in(own_key, 6)
    for position, shards_of in cuts:
        draws = jnp.exp(jax.random.uniform(jax.random.fold_in(own, position), (shards_of,), jnp.float32, smallest / len(cuts), top_value / len(cuts)))
        loudness = loudness * jnp.repeat(draws, shape[position] // shards_of).reshape([-1 if axis == position else 1 for axis in range(len(shape))])
    return loudness


def shared_out(rng, own, number, rows, count, top, most, skew):
    sequence = jax.random.permutation(rng, count)
    crowded, ordinary = portions_of(count, rows * top, most, skew, True), portions_of(count, rows * top, most, skew, False)
    places = jnp.arange(count)

    def named(sizes, turn):
        used = int((sizes > 0).sum())
        fixed = max(1, used // 4)
        passed = fixed + (places - fixed + turn * (used - fixed)) % max(1, count - fixed)
        return jnp.zeros((count,), jnp.int32).at[sequence[jnp.where(places < fixed, places, passed)]].set(jnp.asarray(sizes, jnp.int32))

    sizes = jnp.where(number % 4 == 0, named(crowded, number // 4), named(ordinary, number - number // 4 - 1))
    mixed = jax.random.permutation(jax.random.fold_in(own, 3), count)
    giver, sink = mixed[0:count // 2 * 2:2], mixed[1:count // 2 * 2:2]
    margin = jnp.minimum(sizes[giver] - 1, most - sizes[sink]) // 2
    margin = jnp.where((giver == sequence[0]) | (sink == sequence[0]) | (sizes[sink] == 0), 0, jnp.maximum(margin, 0))
    passed = jax.random.randint(jax.random.fold_in(own, 4), (count // 2,), 0, 1 << 20) % (margin + 1)
    sizes = sizes.at[giver].add(-passed).at[sink].add(passed)
    items = jnp.searchsorted(jnp.cumsum(sizes), jnp.arange(rows * top), side="right").astype(jnp.int32)
    listing = items.reshape(top, rows).T
    listing = listing[jax.random.permutation(jax.random.fold_in(own, 1), rows)]
    turn = jax.random.randint(jax.random.fold_in(own, 2), (rows, 1), 0, top)
    return jnp.take_along_axis(listing, (jnp.arange(top)[None, :] + turn) % top, axis=1)


def portions_of(amount, total, reach, lean, full):
    weights = [(1 << 20) // math.isqrt(rank ** lean) + 1 for rank in range(1, amount + 1)]
    largest = reach if full else min(reach, max(-(-total // amount), total * weights[0] // sum(weights)))
    least = 1 if total - largest >= amount - 1 else 0
    counts, spare = [largest] + [least] * (amount - 1), total - largest - least * (amount - 1)
    while spare > 0:
        free = [i for i in range(1, amount) if counts[i] < largest] or [i for i in range(1, amount) if counts[i] < reach]
        mass, budget = sum([weights[i] for i in free]), spare
        for i in free:
            addition = min(reach - counts[i], max(1, budget * weights[i] // mass), spare)
            counts[i] = counts[i] + addition
            spare = spare - addition
    return np.array(counts)


def centred(key, shape, spread, most, shards=(), kind=jnp.bfloat16):
    result = jax.random.normal(key, shape, jnp.float32) * spread
    if len(shards) > 0:
        result = block_levels(key, shape, shards, -0.22, 0.18) * result
    return jnp.clip(result, min=-most, max=most).astype(kind)


def setup_inputs(seed: int = 0) -> dict:
    seeds = jax.random.split(jax.random.key(seed), 7)
    tokens = centred(seeds[0], (TOKENS, D), 1.0, 6.0, ((0, 32),))
    target = centred(seeds[1], (TOKENS, D), 1.0, 6.0, ((0, 32),))
    expert_ids_keys = jax.random.split(jax.random.fold_in(seeds[2], 1), TOKENS // TOK_DEV)
    expert_ids_turns = jax.random.permutation(jax.random.fold_in(seeds[2], 3), TOKENS // TOK_DEV)
    expert_ids = jax.vmap(lambda own, number: shared_out(jax.random.fold_in(seeds[2], 2), own, number, TOK_DEV, EXPERTS, TOPK, CAP, 2))(expert_ids_keys, expert_ids_turns).reshape((TOKENS, TOPK))
    gates = jnp.clip(0.05 + 0.45 * jax.random.uniform(seeds[3], (TOKENS, TOPK), jnp.float32) ** block_levels(seeds[3], (TOKENS, TOPK), ((0, 32),), -0.2, 0.2), 0.05, 0.5)
    w_in = centred(seeds[4], (D, EXPERTS, 2 * H), D ** -0.5, 0.125, ((1, 8),))
    w_out = centred(seeds[5], (H, EXPERTS, D), H ** -0.5, 0.21875, ((1, 8),))
    return dict(tokens=tokens, target=target, expert_ids=expert_ids, gates=gates, w_in=w_in, w_out=w_out)


def swiglu_forward(preact, hidden):
    gate_part = preact[..., :hidden]
    up_part = preact[..., hidden:]
    return gate_part * jax.nn.sigmoid(gate_part) * up_part


def swiglu_backward(preact, upstream, hidden):
    gate_part = preact[..., :hidden]
    up_part = preact[..., hidden:]
    sigmoid_value = jax.nn.sigmoid(gate_part)
    silu_value = gate_part * sigmoid_value
    derivative = sigmoid_value * (1.0 + gate_part * (1.0 - sigmoid_value))
    return jnp.concatenate([upstream * up_part * derivative, upstream * silu_value], axis=-1)


def rounded(value):
    return lax.optimization_barrier(value.astype(jnp.bfloat16)).astype(jnp.float32)


def reference(tokens, target, expert_ids, gates, w_in, w_out):
    per_replica = TOK_DEV * N_EXPERT
    limit = N_EXPERT * CAP
    flat_ids = expert_ids.reshape(N_DP, per_replica * TOPK)
    gate_flat = gates.reshape(N_DP, per_replica * TOPK)
    token_rows = tokens.reshape(N_DP, per_replica, D)
    weights_in = jnp.transpose(w_in, (1, 0, 2))
    weights_out = jnp.transpose(w_out, (1, 0, 2))
    expert_list = jnp.arange(EXPERTS, dtype=jnp.int32)

    def gather_routes(replica, expert):
        matches = flat_ids[replica] == expert
        found = jnp.nonzero(matches, size=limit, fill_value=0)[0].astype(jnp.int32)
        live = (jnp.arange(limit, dtype=jnp.int32) < jnp.sum(matches.astype(jnp.int32)))[:, None]
        owners = found // TOPK
        rows = jnp.where(live, token_rows[replica][owners], jnp.zeros((), jnp.bfloat16))
        return found, owners, live, rows

    def forward_step(mixture, inputs):
        expert, weight_in, weight_out = inputs
        for replica in range(N_DP):
            found, owners, live, rows = gather_routes(replica, expert)
            preact = jnp.dot(rows, weight_in, preferred_element_type=jnp.float32)
            activation = swiglu_forward(preact, H).astype(jnp.bfloat16)
            output = jnp.dot(activation, weight_out, preferred_element_type=jnp.float32).astype(jnp.bfloat16)
            term = jnp.where(live, gate_flat[replica][found][:, None] * output.astype(jnp.float32), 0.0)
            mixture = mixture.at[replica, owners].add(term)
        return mixture, None

    mixture = lax.scan(forward_step, jnp.zeros((N_DP, per_replica, D), jnp.float32),
                       (expert_list, weights_in, weights_out))[0]
    student = token_rows.astype(jnp.float32) + mixture
    residual_grad = student - target.reshape(N_DP, per_replica, D).astype(jnp.float32)

    def backward_step(grad_rows, inputs):
        expert, weight_in, weight_out = inputs
        sum_in = jnp.zeros((D, 2 * H), jnp.float32)
        sum_out = jnp.zeros((H, D), jnp.float32)
        for replica in range(N_DP):
            found, owners, live, rows = gather_routes(replica, expert)
            preact = jnp.dot(rows, weight_in, preferred_element_type=jnp.float32)
            activation = swiglu_forward(preact, H).astype(jnp.bfloat16)
            scaled = jnp.where(live, (gate_flat[replica][found][:, None] * residual_grad[replica][owners]).astype(jnp.bfloat16),
                               jnp.zeros((), jnp.bfloat16))
            act_grad = jnp.dot(scaled, weight_out.T, preferred_element_type=jnp.float32)
            pre_grad = swiglu_backward(preact, act_grad, H).astype(jnp.bfloat16)
            input_grad = jnp.dot(pre_grad, weight_in.T, preferred_element_type=jnp.float32).astype(jnp.bfloat16)
            grad_rows = grad_rows.at[replica, owners].add(jnp.where(live, input_grad.astype(jnp.float32), 0.0))
            sum_in = sum_in + rounded(jnp.dot(rows.T, pre_grad, preferred_element_type=jnp.float32))
            sum_out = sum_out + rounded(jnp.dot(activation.T, scaled, preferred_element_type=jnp.float32))
        return grad_rows, (sum_in.astype(jnp.bfloat16), sum_out.astype(jnp.bfloat16))

    grad_rows, stacked = lax.scan(backward_step, residual_grad, (expert_list, weights_in, weights_out))
    grad_tokens = grad_rows.astype(jnp.bfloat16).reshape(TOKENS, D)
    grad_in = jnp.transpose(stacked[0], (1, 0, 2))
    grad_out = jnp.transpose(stacked[1], (1, 0, 2))
    return grad_tokens, grad_in, grad_out
```

```python
import jax
import jax.numpy as jnp
from jax import lax
from jax.sharding import PartitionSpec as P


def swiglu_forward(preact, hidden):
    gate_part = preact[..., :hidden]
    up_part = preact[..., hidden:]
    return gate_part * jax.nn.sigmoid(gate_part) * up_part


def swiglu_backward(preact, upstream, hidden):
    gate_part = preact[..., :hidden]
    up_part = preact[..., hidden:]
    sigmoid_value = jax.nn.sigmoid(gate_part)
    silu_value = gate_part * sigmoid_value
    derivative = sigmoid_value * (1.0 + gate_part * (1.0 - sigmoid_value))
    return jnp.concatenate([upstream * up_part * derivative, upstream * silu_value], axis=-1)


def dot32(spec, left, right):
    return jnp.einsum(spec, left, right, preferred_element_type=jnp.float32)


def per_device(tokens, target, expert_ids, gates, w_in, w_out):
    tok_rows, model_width = tokens.shape
    route_count = expert_ids.shape[1]
    hidden = w_out.shape[0]
    local_experts = w_in.shape[1]
    peers = lax.axis_size("expert")
    experts_all = local_experts * peers
    capacity = 3 * tok_rows * route_count // (2 * experts_all)
    slots = -(-capacity // 16) * 16
    rows = peers * slots

    block = lax.all_gather(tokens, "expert")
    ids = lax.all_gather(expert_ids, "expert")
    weights = lax.all_gather(gates, "expert")
    first = lax.axis_index("expert") * local_experts
    picks, slot_gates = [], []
    for e in range(local_experts):
        named = ids == first + e
        member = jnp.any(named, axis=2)
        gate = jnp.sum(jnp.where(named, weights, 0.0), axis=2)
        place = jnp.cumsum(member.astype(jnp.int32), axis=1) - 1
        place = jnp.where(member, place, -1)
        pick = place[:, None, :] == jnp.arange(slots, dtype=jnp.int32)[None, :, None]
        picks.append(pick.astype(jnp.bfloat16))
        slot_gates.append(
            jnp.sum(jnp.where(pick, gate[:, None, :], 0.0), axis=2).reshape(rows, 1)
        )
    pick_all = jnp.concatenate(picks, axis=1)

    def dispatch(e, blocks):
        return dot32("bst,btd->bsd", picks[e], blocks).reshape(rows, model_width)

    def combine(parts):
        stacked = jnp.concatenate(
            [part.reshape(peers, slots, model_width) for part in parts], axis=1
        )
        total = dot32("bst,bsd->btd", pick_all, stacked).astype(jnp.bfloat16)
        return lax.psum_scatter(
            total.reshape(peers * tok_rows, model_width), "expert", scatter_dimension=0, tiled=True
        ).astype(jnp.float32)

    weights_in = [w_in[:, e, :] for e in range(local_experts)]
    weights_out = [w_out[:, e, :] for e in range(local_experts)]

    sent, preacts, activations, outputs = [], [], [], []
    for e in range(local_experts):
        sent.append(dispatch(e, block).astype(jnp.bfloat16))
        preacts.append(dot32("sd,dh->sh", sent[e], weights_in[e]))
        activations.append(swiglu_forward(preacts[e], hidden).astype(jnp.bfloat16))
        outputs.append(
            (dot32("sh,hd->sd", activations[e], weights_out[e]) * slot_gates[e]).astype(
                jnp.bfloat16
            )
        )
    student = tokens.astype(jnp.float32) + combine(outputs)
    residual_grad = student - target.astype(jnp.float32)

    grad_block = lax.all_gather(residual_grad.astype(jnp.bfloat16), "expert")
    input_grads, terms_in, terms_out = [], [], []
    for e in range(local_experts):
        scaled = (dispatch(e, grad_block) * slot_gates[e]).astype(jnp.bfloat16)
        terms_out.append(dot32("sh,sd->hd", activations[e], scaled).astype(jnp.bfloat16))
        act_grad = dot32("sd,hd->sh", scaled, weights_out[e])
        pre_grad = swiglu_backward(preacts[e], act_grad, hidden).astype(jnp.bfloat16)
        terms_in.append(dot32("sd,sh->dh", sent[e], pre_grad).astype(jnp.bfloat16))
        input_grads.append(dot32("sh,dh->sd", pre_grad, weights_in[e]).astype(jnp.bfloat16))
    grad_out = [
        lax.psum_scatter(term, "dp", scatter_dimension=1, tiled=True) for term in terms_out
    ]
    grad_in = [lax.psum_scatter(term, "dp", scatter_dimension=0, tiled=True) for term in terms_in]
    grad_tokens = (residual_grad + combine(input_grads)).astype(jnp.bfloat16)
    return grad_tokens, jnp.stack(grad_in, axis=1), jnp.stack(grad_out, axis=1)


def solution(mesh):
    in_specs = (
        P(("dp", "expert"), None),
        P(("dp", "expert"), None),
        P(("dp", "expert"), None),
        P(("dp", "expert"), None),
        P(None, "expert", None),
        P(None, "expert", None),
    )
    out_specs = (P(("dp", "expert"), None), P("dp", "expert", None), P(None, "expert", "dp"))
    return jax.shard_map(
        per_device, mesh=mesh, in_specs=in_specs, out_specs=out_specs, check_vma=False
    )
```
